32 devices in a mesh: groups: 2 (over y), leaf: 4 (over z), sub: 4 (over x, core).
Axes of the slice: x: 2, y: 2, z: 4, core: 2. Of those that a mesh axis runs over, the one named last changes fastest.
Arguments:
- noise: float32 [512, 16384], P('groups', ('leaf', 'sub')), parts along dimension 0, may hold values from -6 to 6
- leaf_blocks: bfloat16 [8, 4096, 4096], P(('groups', 'leaf'), 'sub'), parts along dimension 0, may hold values from -0.09375 to 0.09375
- proj_basis: float32 [4, 64, 16384], P('groups', None, ('leaf', 'sub')), parts along dimension 0, may hold values from -0.09375 to 0.09375, as said below
- expand_basis: float32 [4, 64, 16384], P('groups', None, ('leaf', 'sub')), parts along dimension 0, may hold values from -0.75 to 0.75
Outputs:
- perturbation: float32 [512, 16384], P('groups', ('leaf', 'sub')), parts along dimension 0
The draws below stay inside these ranges and needn't reach their ends.
There are 2 independent parts, one for each index of `groups`. The reference program is written for one: setup_inputs(seed, part) draws one part's arguments, and reference() takes and returns one part's arrays. A program takes and returns all parts, laid end to end along the dimension named above; each array names one. Nothing has to cross between parts.
Inputs may be any that keep to these rules, and one draw needn't show every extreme that they name: `proj_basis`: entries of level l are at most 6 * (4096 * 2**l) ** -0.5 in magnitude.
All inputs are finite; a program needn't handle non-finite values.
Results may differ from the reference program's by a relative error of at most 0.0017.
Values may be sent and summed in bfloat16 or wider, within the bound.
A program may use at most 64 MiB of HBM per device.

```python
import jax
import jax.numpy as jnp
from jax import lax

LEAF = 4096
RANK = 64
NVEC = 256
LEAVES = 4
LEVELS = 2
POINTS = 16384


def draw_proj_basis(key, part):
    key = jax.random.fold_in(key, 11)
    shape = (LEVELS, RANK, POINTS)
    values = jnp.clip(jax.random.normal(key, shape, jnp.float32), -6.0, 6.0)
    level_ids = jnp.arange(LEVELS, dtype=jnp.float32).reshape(LEVELS, 1, 1)
    scales = (LEAF * jnp.exp2(level_ids)) ** (-0.5)
    return values * scales


def steps_of(key, extent, shards, smallest, top_value):
    factor_of = 1.0
    for dim, shards_of in shards:
        steps = jax.random.uniform(jax.random.fold_in(jax.random.fold_in(key, 6), dim), (shards_of,), jnp.float32, smallest / len(shards), top_value / len(shards))
        factor_of = factor_of * jnp.repeat(jnp.exp(steps), extent[dim] // shards_of).reshape((-1,) + (1,) * (len(extent) - 1 - dim))
    return factor_of


def bell_draw(key, shape, spread, reach, cuts=(), kind=jnp.bfloat16):
    array = spread * jax.random.normal(key, shape, jnp.float32)
    if cuts:
        array = array * steps_of(key, shape, cuts, -0.22, 0.18)
    return jnp.clip(array, -reach, reach).astype(kind)


def setup_inputs(seed: int = 0, part: int = 0) -> dict:
    key_of = jax.random.split(jax.random.key(seed), 5)
    own_keys = jax.random.split(jax.random.fold_in(key_of[4], part), 5)
    return {
        "noise": bell_draw(own_keys[0], (NVEC, POINTS), 1.0, 6.0, ((1, 16),), jnp.float32),
        "leaf_blocks": bell_draw(own_keys[1], (LEAVES, LEAF, LEAF), LEAF ** -0.5, 0.09375, ((0, 4), (1, 4))),
        "proj_basis": draw_proj_basis(jax.random.fold_in(jax.random.fold_in(key_of[4], part), 71), part),
        "expand_basis": bell_draw(own_keys[3], (LEVELS, RANK, POINTS), RANK ** -0.5, 0.75, ((2, 16),), jnp.float32),
    }


def leaf_product(pair):
    block, piece = pair
    return lax.dot_general(piece, block, (((1,), (1,)), ((), ())), preferred_element_type=jnp.float32)


def reference(noise, leaf_blocks, proj_basis, expand_basis):
    noise_b = noise.astype(jnp.bfloat16)
    pieces = noise_b.reshape(NVEC, LEAVES, LEAF).transpose(1, 0, 2)
    near = lax.map(leaf_product, (leaf_blocks, pieces))
    total = near.transpose(1, 0, 2).reshape(NVEC, POINTS)
    for level in range(LEVELS):
        nodes = LEAVES // (2 ** level)
        width = LEAF * (2 ** level)
        coeff = jnp.einsum("rnm,vnm->nrv", proj_basis[level].reshape(RANK, nodes, width), noise.reshape(NVEC, nodes, width), precision=lax.Precision.HIGHEST)
        other = coeff.reshape(nodes // 2, 2, RANK, NVEC)[:, ::-1].reshape(nodes, RANK, NVEC)
        added = jnp.einsum("nrv,rnm->vnm", other, expand_basis[level].reshape(RANK, nodes, width), precision=lax.Precision.HIGHEST)
        total = total + added.reshape(NVEC, POINTS)
    return total
```

```python
import functools

import jax
import jax.numpy as jnp
from jax import lax
from jax.experimental import pallas as pl
from jax.experimental.pallas import tpu as pltpu
from jax.sharding import PartitionSpec as P

MESH = pl.DeviceIdType.MESH
CHUNKS = 8
WINDOW = 2
TILE = 256


def split(value):
    high = value.astype(jnp.bfloat16)
    return high, (value - high.astype(jnp.float32)).astype(jnp.bfloat16)


def dot(a, b, da, db):
    return lax.dot_general(a, b, (((da,), (db,)), ((), ())), preferred_element_type=jnp.float32)


def kernel(
    subs, levels, noise_hbm, block_hbm, proj_hbm, expand_hbm, out_hbm,
    noise, low, gat, blk, proj, expand, acc, parts, got_a, chip, got_b, run, got_c, co,
    ld, ld_blk, out_sem, own_s, own_r, x_s, x_r, f_s, a_s, a_r, b_s, b_r, c_s, c_r, d_s, d_r, e_s,
):
    chips = subs // 2
    chunks, vecs, kc = gat.shape[1:]
    points = chunks * kc
    rank = proj.shape[1]
    share = rank // subs
    tiles, _, tile = acc.shape
    me = lax.axis_index("sub")
    leaf = lax.axis_index("leaf")
    core = lax.rem(me, 2)
    x = me // 2
    mate = me + 1 - 2 * core

    def chip_at(d):
        return lax.rem(x + d, chips)

    def chip_from(d):
        return lax.rem(x + chips - d, chips)

    def leaf_mate(level):
        bit = lax.rem(leaf // 2**level, 2)
        return leaf + 2**level * (1 - 2 * bit)

    def remote(src, dst, send, recv, **device):
        return pltpu.make_async_remote_copy(
            src_ref=src, dst_ref=dst, send_sem=send, recv_sem=recv, device_id=device, device_id_type=MESH
        )

    loads = [
        pltpu.make_async_copy(noise_hbm, noise, ld.at[0]),
        pltpu.make_async_copy(proj_hbm, proj, ld.at[1]),
        pltpu.make_async_copy(expand_hbm, expand, ld.at[2]),
    ]

    def load_blk(j):
        columns = pl.ds(pl.multiple_of(j * points, points), points)
        return pltpu.make_async_copy(block_hbm.at[0, :, columns], blk.at[j], ld_blk.at[j])

    loads[0].start()
    loads[1].start()
    load_blk(me).start()
    load_blk(mate).start()
    loads[2].start()
    for d in range(1, chips):
        for c in (core, 1 - core):
            load_blk(chip_from(d) * 2 + c).start()

    barrier = pltpu.get_barrier_semaphore()
    pl.semaphore_signal(barrier, inc=1, device_id={"sub": mate}, device_id_type=MESH)
    for d in range(1, chips):
        pl.semaphore_signal(barrier, inc=1, device_id={"sub": chip_at(d) * 2 + core}, device_id_type=MESH)
    for level in range(levels):
        pl.semaphore_signal(barrier, inc=1, device_id={"leaf": leaf_mate(level)}, device_id_type=MESH)

    loads[0].wait()
    for k in range(chunks):
        piece = noise[:, k * kc : (k + 1) * kc]
        gat[me, k], low[:, k * kc : (k + 1) * kc] = split(piece)

    pl.semaphore_wait(barrier, chips + levels)

    sends = []

    def go(copy):
        copy.start()
        sends.append(copy)
        return copy

    def send_x(d, k):
        return remote(gat.at[me, k], gat.at[me, k], x_s.at[d, k], x_r.at[me, k], sub=chip_at(d) * 2 + core)

    x_sent = {}
    for k in range(min(WINDOW, chunks)):
        for d in range(1, chips):
            x_sent[d, k] = send_x(d, k)
            x_sent[d, k].start()
    own = go(remote(gat.at[me], gat.at[me], own_s, own_r, sub=mate))

    loads[1].wait()
    high = jnp.concatenate([gat[me, k] for k in range(chunks)], axis=1)
    p_high, p_low = split(proj[...].reshape(levels * rank, points))
    both = dot(jnp.concatenate([p_high, p_low], axis=0), high, 1, 1)
    part = both[: levels * rank] + both[levels * rank :] + dot(p_high, low[...], 1, 1)
    for j in range(subs):
        for level in range(levels):
            first = level * rank + j * share
            parts[j % 2, j // 2, level] = part[first : first + share]
    a = go(remote(parts.at[1 - core], got_a, a_s, a_r, sub=mate))

    def near(j, ks, init=False):
        lhs = jnp.concatenate([gat[j, k] for k in ks], axis=1)
        lanes = slice(ks[0] * kc, (ks[-1] + 1) * kc)

        def step(t, _):
            rows = pl.ds(pl.multiple_of(t * tile, tile), tile)
            product = dot(lhs, blk[j, rows, lanes], 1, 1)
            if init:
                acc[t] = product
            else:
                acc[t] += product
            return 0

        lax.fori_loop(0, tiles, step, 0, unroll=False)

    every = list(range(chunks))
    load_blk(me).wait()
    near(me, every, init=True)

    a.wait_recv()
    chip[...] = parts[core] + got_a[...]
    for d in range(1, chips):
        go(remote(chip.at[chip_at(d)], got_b.at[x], b_s.at[d], b_r.at[x], sub=chip_at(d) * 2 + core))

    own.wait_recv()
    load_blk(mate).wait()
    near(mate, every)

    def recv_b():
        total = chip[x]
        for d in range(1, chips):
            src = chip_from(d)
            remote(chip.at[src], got_b.at[src], b_s.at[d], b_r.at[src], sub=mate).wait_recv()
            total = total + got_b[src]
        run[0] = total
        send_c(0)

    c_copies = {}

    def send_c(level):
        c_copies[level] = go(
            remote(
                run.at[level, pl.ds(level, levels - level)],
                got_c.at[level, pl.ds(level, levels - level)],
                c_s.at[level],
                c_r.at[level],
                leaf=leaf_mate(level),
            )
        )

    def recv_c(level):
        c_copies[level].wait_recv()
        co[me, level] = got_c[level, level]
        if level + 1 < levels:
            run[level + 1, level + 1 :] = run[level, level + 1 :] + got_c[level, level + 1 :]
            send_c(level + 1)
        else:
            for d in range(1, chips):
                go(remote(co.at[me], co.at[me], d_s.at[d], d_r.at[me], sub=chip_at(d) * 2 + core))
            go(remote(co.at[me], co.at[me], d_s.at[0], d_r.at[me], sub=mate))

    def recv_d():
        for d in range(1, chips):
            src = chip_from(d) * 2 + core
            remote(co.at[src], co.at[src], d_s.at[d], d_r.at[src], sub=mate).wait_recv()
            go(remote(co.at[src], co.at[src], e_s.at[d], d_r.at[src], sub=mate))

    events = [recv_b] + [functools.partial(recv_c, level) for level in range(levels)] + [recv_d]
    slots = {}
    for i, event in enumerate(events):
        slots.setdefault(max(0, chunks - 1 - len(events) + i), []).append(event)

    for d in range(1, chips):
        load_blk(chip_from(d) * 2 + core).wait()
        load_blk(chip_from(d) * 2 + 1 - core).wait()

    for k in range(chunks):
        for d in range(1, chips):
            src = chip_from(d) * 2 + core
            remote(gat.at[src, k], gat.at[src, k], x_s.at[d, k], x_r.at[src, k], sub=mate).wait_recv()
            go(remote(gat.at[src, k], gat.at[src, k], f_s.at[d, k], x_r.at[src, k], sub=mate))
        for d in range(1, chips):
            x_sent[d, k].wait_send()
            if k + WINDOW < chunks:
                x_sent[d, k + WINDOW] = send_x(d, k + WINDOW)
                x_sent[d, k + WINDOW].start()
        for event in slots.get(k, []):
            event()
        for d in range(1, chips):
            near(chip_from(d) * 2 + core, [k])
        if k == chunks - 1:
            break
        for d in range(1, chips):
            src = chip_from(d) * 2 + 1 - core
            remote(gat.at[src, k], gat.at[src, k], x_s.at[d, k], x_r.at[src, k], sub=mate).wait_recv()
            near(src, [k])

    remote(co.at[mate], co.at[mate], d_s.at[0], d_r.at[mate], sub=mate).wait_recv()
    for d in range(1, chips):
        src = chip_from(d) * 2 + 1 - core
        remote(co.at[src], co.at[src], d_s.at[0], d_r.at[src], sub=mate).wait_recv()
    loads[2].wait()
    coeff = jnp.concatenate([co[j, level] for level in range(levels) for j in range(subs)], axis=0)
    c_high, c_low = split(coeff)
    lhs = jnp.concatenate([c_high, c_high, c_low], axis=0)
    for t in range(tiles):
        e_high, e_low = split(expand[:, :, t * tile : (t + 1) * tile].reshape(levels * rank, tile))
        acc[t] += dot(lhs, jnp.concatenate([e_high, e_low, e_high], axis=0), 0, 0)

    k = chunks - 1
    for d in range(1, chips):
        src = chip_from(d) * 2 + 1 - core
        remote(gat.at[src, k], gat.at[src, k], x_s.at[d, k], x_r.at[src, k], sub=mate).wait_recv()
    outs = []
    for t in range(tiles):
        total = acc[t]
        for d in range(1, chips):
            src = chip_from(d) * 2 + 1 - core
            total = total + dot(gat[src, k], blk[src, t * tile : (t + 1) * tile, k * kc : (k + 1) * kc], 1, 1)
        acc[t] = total
        copy = pltpu.make_async_copy(acc.at[t], out_hbm.at[:, t * tile : (t + 1) * tile], out_sem.at[t])
        copy.start()
        outs.append(copy)

    for copy in sends:
        copy.wait_send()
    for copy in outs:
        copy.wait()


def solution(mesh):
    subs = mesh.shape["sub"]
    chips = subs // 2

    def shards(noise, leaf_blocks, proj_basis, expand_basis):
        vecs, points = noise.shape
        levels, rank = proj_basis.shape[:2]
        chunks = CHUNKS if points // CHUNKS >= 128 else points // 128
        kc = points // chunks
        tile = min(TILE, points)
        tiles = points // tile
        share = rank // subs
        f32, bf16 = jnp.float32, jnp.bfloat16
        dma = pltpu.SemaphoreType.DMA
        part = (levels, share, vecs)
        return pl.pallas_call(
            functools.partial(kernel, subs, levels),
            out_shape=jax.ShapeDtypeStruct((vecs, points), f32),
            in_specs=[pl.BlockSpec(memory_space=pl.ANY)] * 4,
            out_specs=pl.BlockSpec(memory_space=pl.ANY),
            scratch_shapes=[
                pltpu.VMEM((vecs, points), f32),
                pltpu.VMEM((vecs, points), bf16),
                pltpu.VMEM((subs, chunks, vecs, kc), bf16),
                pltpu.VMEM((subs, points, points), bf16),
                pltpu.VMEM((levels, rank, points), f32),
                pltpu.VMEM((levels, rank, points), f32),
                pltpu.VMEM((tiles, vecs, tile), f32),
                pltpu.VMEM((2, chips) + part, f32),
                pltpu.VMEM((chips,) + part, f32),
                pltpu.VMEM((chips,) + part, f32),
                pltpu.VMEM((chips,) + part, f32),
                pltpu.VMEM((levels,) + part, f32),
                pltpu.VMEM((levels,) + part, f32),
                pltpu.VMEM((subs,) + part, f32),
                dma((3,)),
                dma((subs,)),
                dma((tiles,)),
                dma, dma,
                dma((chips, chunks)),
                dma((subs, chunks)),
                dma((chips, chunks)),
                dma, dma,
                dma((chips,)),
                dma((chips,)),
                dma((levels,)),
                dma((levels,)),
                dma((chips,)),
                dma((subs,)),
                dma((chips,)),
            ],
            compiler_params=pltpu.CompilerParams(
                collective_id=0, has_side_effects=True, vmem_limit_bytes=48 * 2**20
            ),
        )(noise, leaf_blocks, proj_basis, expand_basis)

    return jax.shard_map(
        shards,
        mesh=mesh,
        in_specs=(
            P("groups", ("leaf", "sub")),
            P(("groups", "leaf"), "sub", None),
            P("groups", None, ("leaf", "sub")),
            P("groups", None, ("leaf", "sub")),
        ),
        out_specs=P("groups", ("leaf", "sub")),
        check_vma=False,
    )
```

```python
import functools

import jax
import jax.numpy as jnp
from jax import lax
from jax.experimental import pallas as pl
from jax.experimental.pallas import tpu as pltpu
from jax.sharding import PartitionSpec as P

MESH = pl.DeviceIdType.MESH
CHUNKS = 8
TILE = 256
LIMIT = 63 * 2**20


def split(value):
    high = value.astype(jnp.bfloat16)
    return high, (value - high.astype(jnp.float32)).astype(jnp.bfloat16)


def dot(a, b, da, db):
    return lax.dot_general(a, b, (((da,), (db,)), ((), ())), preferred_element_type=jnp.float32)


def kernel(
    subs, levels, noise_hbm, block_hbm, proj_hbm, expand_hbm, out_hbm,
    noise, low, gat, blk, proj, expand, acc, parts, got_a, chip, got_b, run, got_c, co,
    ld, ld_blk, out_sem, own_s, own_r, x_s, x_r, f_s, a_s, a_r, b_s, b_r, c_s, c_r, d_s, d_r,
):
    chips = subs // 2
    chunks, vecs, kc = gat.shape[1:]
    points = chunks * kc
    rank = proj.shape[1]
    half = rank // 2
    tiles, _, tile = acc.shape
    me = lax.axis_index("sub")
    leaf = lax.axis_index("leaf")
    core = lax.rem(me, 2)
    x = me // 2
    mate = me + 1 - 2 * core

    def chip_at(d):
        return lax.rem(x + d, chips)

    def chip_from(d):
        return lax.rem(x + chips - d, chips)

    def leaf_mate(level):
        bit = lax.rem(leaf // 2**level, 2)
        return leaf + 2**level * (1 - 2 * bit)

    def remote(src, dst, send, recv, **device):
        return pltpu.make_async_remote_copy(
            src_ref=src, dst_ref=dst, send_sem=send, recv_sem=recv, device_id=device, device_id_type=MESH
        )

    loads = [
        pltpu.make_async_copy(noise_hbm, noise, ld.at[0]),
        pltpu.make_async_copy(proj_hbm, proj, ld.at[1]),
        pltpu.make_async_copy(expand_hbm, expand, ld.at[2]),
    ]

    def load_blk(j):
        columns = pl.ds(pl.multiple_of(j * points, points), points)
        return pltpu.make_async_copy(block_hbm.at[0, :, columns], blk.at[j], ld_blk.at[j])

    barrier = pltpu.get_barrier_semaphore()
    pl.semaphore_signal(barrier, inc=1, device_id={"sub": mate}, device_id_type=MESH)
    for d in range(1, chips):
        pl.semaphore_signal(barrier, inc=1, device_id={"sub": chip_at(d) * 2 + core}, device_id_type=MESH)
    for level in range(levels):
        pl.semaphore_signal(barrier, inc=1, device_id={"leaf": leaf_mate(level)}, device_id_type=MESH)

    loads[0].start()
    loads[1].start()
    load_blk(me).start()
    load_blk(mate).start()
    loads[2].start()
    for d in range(1, chips):
        for c in (core, 1 - core):
            load_blk(chip_from(d) * 2 + c).start()

    loads[0].wait()
    for k in range(chunks):
        piece = noise[:, k * kc : (k + 1) * kc]
        gat[me, k], low[:, k * kc : (k + 1) * kc] = split(piece)

    loads[1].wait()
    high = jnp.concatenate([gat[me, k] for k in range(chunks)], axis=1)
    p_high, p_low = split(proj[...].reshape(levels * rank, points))
    both = dot(jnp.concatenate([p_high, p_low], axis=0), high, 1, 1)
    part = both[: levels * rank] + both[levels * rank :] + dot(p_high, low[...], 1, 1)
    for c in range(2):
        for level in range(levels):
            first = level * rank + c * half
            parts[c, level] = part[first : first + half]

    sends = []

    def go(copy):
        copy.start()
        sends.append(copy)
        return copy

    def near(j, ks, init=False):
        lhs = jnp.concatenate([gat[j, k] for k in ks], axis=1)
        lanes = slice(ks[0] * kc, (ks[-1] + 1) * kc)

        def step(t, _):
            rows = pl.ds(pl.multiple_of(t * tile, tile), tile)
            product = dot(lhs, blk[j, rows, lanes], 1, 1)
            if init:
                acc[t] = product
            else:
                acc[t] += product
            return 0

        lax.fori_loop(0, tiles, step, 0, unroll=False)

    def send_x(k):
        for d in range(1, chips):
            go(remote(gat.at[me, k], gat.at[me, k], x_s.at[d, k], x_r.at[me, k], sub=chip_at(d) * 2 + core))

    pl.semaphore_wait(barrier, chips + levels)
    a = go(remote(parts.at[1 - core], got_a, a_s, a_r, sub=mate))
    send_x(0)
    own = go(remote(gat.at[me], gat.at[me], own_s, own_r, sub=mate))

    a.wait_recv()
    chip[...] = parts[core] + got_a[...]
    for d in range(1, chips):
        go(remote(chip, got_b.at[x], b_s.at[d], b_r.at[x], sub=chip_at(d) * 2 + core))
    for k in range(1, chunks):
        send_x(k)

    every = list(range(chunks))
    load_blk(me).wait()
    near(me, every, init=True)
    own.wait_recv()
    load_blk(mate).wait()
    near(mate, every)

    c_copies = {}

    def send_c(level):
        more = levels - level - 1
        rows = [(0, pl.ds(level + 1, more))] if more else []
        for which, at in rows + [(1, pl.ds(level, 1))]:
            c_copies[level, which] = go(
                remote(
                    run.at[level, at],
                    got_c.at[level, at],
                    c_s.at[level, which],
                    c_r.at[level, which],
                    leaf=leaf_mate(level),
                )
            )

    def recv_b():
        total = chip[...]
        for d in range(1, chips):
            src = chip_from(d)
            remote(chip, got_b.at[src], b_s.at[d], b_r.at[src], sub=mate).wait_recv()
            total = total + got_b[src]
        run[0] = total
        send_c(0)

    def recv_c(level):
        if level + 1 < levels:
            c_copies[level, 0].wait_recv()
            run[level + 1, level + 1 :] = run[level, level + 1 :] + got_c[level, level + 1 :]
            send_c(level + 1)
        c_copies[level, 1].wait_recv()
        co[core, level] = got_c[level, level]
        go(remote(co.at[core, level], co.at[core, level], d_s.at[level], d_r.at[level], sub=mate))

    slots = {0: [recv_b]}
    for level in range(levels):
        slots.setdefault(max(0, (level + 1) * chunks // levels - 2), []).append(functools.partial(recv_c, level))

    for d in range(1, chips):
        load_blk(chip_from(d) * 2 + core).wait()
        load_blk(chip_from(d) * 2 + 1 - core).wait()

    for k in range(chunks):
        for d in range(1, chips):
            src = chip_from(d) * 2 + core
            remote(gat.at[src, k], gat.at[src, k], x_s.at[d, k], x_r.at[src, k], sub=mate).wait_recv()
            go(remote(gat.at[src, k], gat.at[src, k], f_s.at[d, k], x_r.at[src, k], sub=mate))
        for event in slots.get(k, []):
            event()
        for d in range(1, chips):
            near(chip_from(d) * 2 + core, [k])
        if k == chunks - 1:
            break
        for d in range(1, chips):
            src = chip_from(d) * 2 + 1 - core
            remote(gat.at[src, k], gat.at[src, k], x_s.at[d, k], x_r.at[src, k], sub=mate).wait_recv()
            near(src, [k])

    for level in range(levels):
        other = co.at[1 - core, level]
        remote(other, other, d_s.at[level], d_r.at[level], sub=mate).wait_recv()
    loads[2].wait()
    coeff = jnp.concatenate([co[c, level] for level in range(levels) for c in range(2)], axis=0)
    c_high, c_low = split(coeff)
    lhs = jnp.concatenate([c_high, c_high, c_low], axis=0)
    for t in range(tiles):
        e_high, e_low = split(expand[:, :, t * tile : (t + 1) * tile].reshape(levels * rank, tile))
        acc[t] += dot(lhs, jnp.concatenate([e_high, e_low, e_high], axis=0), 0, 0)

    k = chunks - 1
    for d in range(1, chips):
        src = chip_from(d) * 2 + 1 - core
        remote(gat.at[src, k], gat.at[src, k], x_s.at[d, k], x_r.at[src, k], sub=mate).wait_recv()
    outs = []
    for t in range(tiles):
        total = acc[t]
        for d in range(1, chips):
            src = chip_from(d) * 2 + 1 - core
            total = total + dot(gat[src, k], blk[src, t * tile : (t + 1) * tile, k * kc : (k + 1) * kc], 1, 1)
        acc[t] = total
        copy = pltpu.make_async_copy(acc.at[t], out_hbm.at[:, t * tile : (t + 1) * tile], out_sem.at[t])
        copy.start()
        outs.append(copy)

    for copy in sends:
        copy.wait_send()
    for copy in outs:
        copy.wait()


def solution(mesh):
    subs = mesh.shape["sub"]
    chips = subs // 2

    def shards(noise, leaf_blocks, proj_basis, expand_basis):
        vecs, points = noise.shape
        levels, rank = proj_basis.shape[:2]
        chunks = CHUNKS if points // CHUNKS >= 128 else points // 128
        kc = points // chunks
        tile = min(TILE, points)
        tiles = points // tile
        f32, bf16 = jnp.float32, jnp.bfloat16
        dma = pltpu.SemaphoreType.DMA
        part = (levels, rank // 2, vecs)
        return pl.pallas_call(
            functools.partial(kernel, subs, levels),
            out_shape=jax.ShapeDtypeStruct((vecs, points), f32),
            in_specs=[pl.BlockSpec(memory_space=pltpu.HBM)] * 4,
            out_specs=pl.BlockSpec(memory_space=pl.ANY),
            scratch_shapes=[
                pltpu.VMEM((vecs, points), f32),
                pltpu.VMEM((vecs, points), bf16),
                pltpu.VMEM((subs, chunks, vecs, kc), bf16),
                pltpu.VMEM((subs, points, points), bf16),
                pltpu.VMEM((levels, rank, points), f32),
                pltpu.VMEM((levels, rank, points), f32),
                pltpu.VMEM((tiles, vecs, tile), f32),
                pltpu.VMEM((2,) + part, f32),
                pltpu.VMEM(part, f32),
                pltpu.VMEM(part, f32),
                pltpu.VMEM((chips,) + part, f32),
                pltpu.VMEM((levels,) + part, f32),
                pltpu.VMEM((levels,) + part, f32),
                pltpu.VMEM((2,) + part, f32),
                dma((3,)),
                dma((subs,)),
                dma((tiles,)),
                dma, dma,
                dma((chips, chunks)),
                dma((subs, chunks)),
                dma((chips, chunks)),
                dma, dma,
                dma((chips,)),
                dma((chips,)),
                dma((levels, 2)),
                dma((levels, 2)),
                dma((levels,)),
                dma((levels,)),
            ],
            compiler_params=pltpu.CompilerParams(
                collective_id=0, has_side_effects=True, vmem_limit_bytes=LIMIT
            ),
        )(noise, leaf_blocks, proj_basis, expand_basis)

    return jax.shard_map(
        shards,
        mesh=mesh,
        in_specs=(
            P("groups", ("leaf", "sub")),
            P(("groups", "leaf"), "sub", None),
            P("groups", None, ("leaf", "sub")),
            P("groups", None, ("leaf", "sub")),
        ),
        out_specs=P("groups", ("leaf", "sub")),
        check_vma=False,
    )
```

```python
import functools

import jax
import jax.numpy as jnp
from jax import lax
from jax.experimental import pallas as pl
from jax.experimental.pallas import tpu as pltpu
from jax.sharding import PartitionSpec as P

MESH = pl.DeviceIdType.MESH
CHUNKS = 8
TILE = 256
LIMIT = 61 * 2**20


def split(value):
    high = value.astype(jnp.bfloat16)
    return high, (value - high.astype(jnp.float32)).astype(jnp.bfloat16)


def dot(a, b, da, db):
    return lax.dot_general(a, b, (((da,), (db,)), ((), ())), preferred_element_type=jnp.float32)


def kernel(
    subs, levels, noise_hbm, block_hbm, proj_hbm, expand_hbm, out,
    noise, low, gat, blk, proj, expand, acc, parts, got_a, chip, got_b, run, got_c, co,
    ld, ld_blk, own_s, own_r, x_s, x_r, f_s, a_s, a_r, b_s, b_r, c_s, c_r, d_s, d_r,
):
    chips = subs // 2
    chunks, vecs, kc = gat.shape[1:]
    points = chunks * kc
    rank = proj.shape[1]
    half = rank // 2
    tiles, _, tile = acc.shape
    me = lax.axis_index("sub")
    leaf = lax.axis_index("leaf")
    core = lax.rem(me, 2)
    x = me // 2
    mate = me + 1 - 2 * core

    def chip_at(d):
        return lax.rem(x + d, chips)

    def chip_from(d):
        return lax.rem(x + chips - d, chips)

    def leaf_mate(level):
        bit = lax.rem(leaf // 2**level, 2)
        return leaf + 2**level * (1 - 2 * bit)

    def remote(src, dst, send, recv, **device):
        return pltpu.make_async_remote_copy(
            src_ref=src, dst_ref=dst, send_sem=send, recv_sem=recv, device_id=device, device_id_type=MESH
        )

    loads = [
        pltpu.make_async_copy(noise_hbm, noise, ld.at[0]),
        pltpu.make_async_copy(proj_hbm, proj, ld.at[1]),
        pltpu.make_async_copy(expand_hbm, expand, ld.at[2]),
    ]

    def load_blk(j):
        columns = pl.ds(pl.multiple_of(j * points, points), points)
        return pltpu.make_async_copy(block_hbm.at[0, :, columns], blk.at[j], ld_blk.at[j])

    barrier = pltpu.get_barrier_semaphore()
    pl.semaphore_signal(barrier, inc=1, device_id={"sub": mate}, device_id_type=MESH)
    for d in range(1, chips):
        pl.semaphore_signal(barrier, inc=1, device_id={"sub": chip_at(d) * 2 + core}, device_id_type=MESH)
    for level in range(levels):
        pl.semaphore_signal(barrier, inc=1, device_id={"leaf": leaf_mate(level)}, device_id_type=MESH)

    loads[0].start()
    loads[1].start()
    load_blk(me).start()
    load_blk(mate).start()
    loads[2].start()
    for d in range(1, chips):
        for c in (core, 1 - core):
            load_blk(chip_from(d) * 2 + c).start()

    loads[0].wait()
    for k in range(chunks):
        piece = noise[:, k * kc : (k + 1) * kc]
        gat[me, k], low[:, k * kc : (k + 1) * kc] = split(piece)

    loads[1].wait()
    high = jnp.concatenate([gat[me, k] for k in range(chunks)], axis=1)
    p_high, p_low = split(proj[...].reshape(levels * rank, points))
    both = dot(jnp.concatenate([p_high, p_low], axis=0), high, 1, 1)
    part = both[: levels * rank] + both[levels * rank :] + dot(p_high, low[...], 1, 1)
    for c in range(2):
        for level in range(levels):
            first = level * rank + c * half
            parts[c, level] = part[first : first + half]

    sends = []

    def go(copy):
        copy.start()
        sends.append(copy)
        return copy

    def near(j, ks, init=False):
        lhs = jnp.concatenate([gat[j, k] for k in ks], axis=1)
        lanes = slice(ks[0] * kc, (ks[-1] + 1) * kc)

        def step(t, _):
            rows = pl.ds(pl.multiple_of(t * tile, tile), tile)
            product = dot(lhs, blk[j, rows, lanes], 1, 1)
            if init:
                acc[t] = product
            else:
                acc[t] += product
            return 0

        lax.fori_loop(0, tiles, step, 0, unroll=True)

    def send_x(k):
        for d in range(1, chips):
            go(remote(gat.at[me, k], gat.at[me, k], x_s.at[d, k], x_r.at[me, k], sub=chip_at(d) * 2 + core))

    pl.semaphore_wait(barrier, chips + levels)
    a = go(remote(parts.at[1 - core], got_a, a_s, a_r, sub=mate))
    send_x(0)
    own = go(remote(gat.at[me], gat.at[me], own_s, own_r, sub=mate))

    a.wait_recv()
    chip[...] = parts[core] + got_a[...]
    for d in range(1, chips):
        go(remote(chip, got_b.at[x], b_s.at[d], b_r.at[x], sub=chip_at(d) * 2 + core))
    for k in range(1, chunks):
        send_x(k)

    every = list(range(chunks))
    load_blk(me).wait()
    near(me, every, init=True)
    own.wait_recv()
    load_blk(mate).wait()
    near(mate, every)

    c_copies = {}

    def send_c(level):
        more = levels - level - 1
        rows = [(0, pl.ds(level + 1, more))] if more else []
        for which, at in rows + [(1, pl.ds(level, 1))]:
            c_copies[level, which] = go(
                remote(
                    run.at[level, at],
                    got_c.at[level, at],
                    c_s.at[level, which],
                    c_r.at[level, which],
                    leaf=leaf_mate(level),
                )
            )

    def recv_b():
        total = chip[...]
        for d in range(1, chips):
            src = chip_from(d)
            remote(chip, got_b.at[src], b_s.at[d], b_r.at[src], sub=mate).wait_recv()
            total = total + got_b[src]
        run[0] = total
        send_c(0)

    def recv_c(level):
        if level + 1 < levels:
            c_copies[level, 0].wait_recv()
            run[level + 1, level + 1 :] = run[level, level + 1 :] + got_c[level, level + 1 :]
            send_c(level + 1)
        c_copies[level, 1].wait_recv()
        co[core, level] = got_c[level, level]
        go(remote(co.at[core, level], co.at[core, level], d_s.at[level], d_r.at[level], sub=mate))

    slots = {0: [recv_b]}
    for level in range(levels):
        slots.setdefault(max(0, (level + 1) * chunks // levels - 2), []).append(functools.partial(recv_c, level))

    for d in range(1, chips):
        load_blk(chip_from(d) * 2 + core).wait()
        load_blk(chip_from(d) * 2 + 1 - core).wait()

    for k in range(chunks):
        for d in range(1, chips):
            src = chip_from(d) * 2 + core
            remote(gat.at[src, k], gat.at[src, k], x_s.at[d, k], x_r.at[src, k], sub=mate).wait_recv()
            go(remote(gat.at[src, k], gat.at[src, k], f_s.at[d, k], x_r.at[src, k], sub=mate))
        for event in slots.get(k, []):
            event()
        for d in range(1, chips):
            near(chip_from(d) * 2 + core, [k])
        if k == chunks - 1:
            break
        for d in range(1, chips):
            src = chip_from(d) * 2 + 1 - core
            remote(gat.at[src, k], gat.at[src, k], x_s.at[d, k], x_r.at[src, k], sub=mate).wait_recv()
            near(src, [k])

    for level in range(levels):
        other = co.at[1 - core, level]
        remote(other, other, d_s.at[level], d_r.at[level], sub=mate).wait_recv()
    loads[2].wait()
    coeff = jnp.concatenate([co[c, level] for level in range(levels) for c in range(2)], axis=0)
    c_high, c_low = split(coeff)
    lhs = jnp.concatenate([c_high, c_high, c_low], axis=0)
    for t in range(tiles):
        e_high, e_low = split(expand[:, :, t * tile : (t + 1) * tile].reshape(levels * rank, tile))
        acc[t] += dot(lhs, jnp.concatenate([e_high, e_low, e_high], axis=0), 0, 0)

    k = chunks - 1
    for d in range(1, chips):
        src = chip_from(d) * 2 + 1 - core
        remote(gat.at[src, k], gat.at[src, k], x_s.at[d, k], x_r.at[src, k], sub=mate).wait_recv()
    for t in range(tiles):
        total = acc[t]
        for d in range(1, chips):
            src = chip_from(d) * 2 + 1 - core
            total = total + dot(gat[src, k], blk[src, t * tile : (t + 1) * tile, k * kc : (k + 1) * kc], 1, 1)
        out[:, t * tile : (t + 1) * tile] = total

    for copy in sends:
        copy.wait_send()


def solution(mesh):
    subs = mesh.shape["sub"]
    chips = subs // 2

    def shards(noise, leaf_blocks, proj_basis, expand_basis):
        vecs, points = noise.shape
        levels, rank = proj_basis.shape[:2]
        chunks = CHUNKS if points // CHUNKS >= 128 else points // 128
        kc = points // chunks
        tile = min(TILE, points)
        tiles = points // tile
        f32, bf16 = jnp.float32, jnp.bfloat16
        dma = pltpu.SemaphoreType.DMA
        part = (levels, rank // 2, vecs)
        return pl.pallas_call(
            functools.partial(kernel, subs, levels),
            out_shape=pltpu.VMEM((vecs, points), f32),
            in_specs=[pl.BlockSpec(memory_space=pltpu.HBM)] * 4,
            out_specs=pl.BlockSpec(memory_space=pltpu.VMEM),
            scratch_shapes=[
                pltpu.VMEM((vecs, points), f32),
                pltpu.VMEM((vecs, points), bf16),
                pltpu.VMEM((subs, chunks, vecs, kc), bf16),
                pltpu.VMEM((subs, points, points), bf16),
                pltpu.VMEM((levels, rank, points), f32),
                pltpu.VMEM((levels, rank, points), f32),
                pltpu.VMEM((tiles, vecs, tile), f32),
                pltpu.VMEM((2,) + part, f32),
                pltpu.VMEM(part, f32),
                pltpu.VMEM(part, f32),
                pltpu.VMEM((chips,) + part, f32),
                pltpu.VMEM((levels,) + part, f32),
                pltpu.VMEM((levels,) + part, f32),
                pltpu.VMEM((2,) + part, f32),
                dma((3,)),
                dma((subs,)),
                dma, dma,
                dma((chips, chunks)),
                dma((subs, chunks)),
                dma((chips, chunks)),
                dma, dma,
                dma((chips,)),
                dma((chips,)),
                dma((levels, 2)),
                dma((levels, 2)),
                dma((levels,)),
                dma((levels,)),
            ],
            compiler_params=pltpu.CompilerParams(
                collective_id=0, has_side_effects=True, vmem_limit_bytes=LIMIT
            ),
        )(noise, leaf_blocks, proj_basis, expand_basis)

    return jax.shard_map(
        shards,
        mesh=mesh,
        in_specs=(
            P("groups", ("leaf", "sub")),
            P(("groups", "leaf"), "sub", None),
            P("groups", None, ("leaf", "sub")),
            P("groups", None, ("leaf", "sub")),
        ),
        out_specs=P("groups", ("leaf", "sub")),
        check_vma=False,
    )
```

```python
import functools

import jax
import jax.numpy as jnp
from jax import lax
from jax.experimental import pallas as pl
from jax.experimental.pallas import tpu as pltpu
from jax.sharding import PartitionSpec as P

MESH = pl.DeviceIdType.MESH
CHUNKS = 8
EARLY = 1
TILE = 256
LIMIT = 61 * 2**20


def split(value):
    high = value.astype(jnp.bfloat16)
    return high, (value - high.astype(jnp.float32)).astype(jnp.bfloat16)


def dot(a, b, da, db):
    return lax.dot_general(a, b, (((da,), (db,)), ((), ())), preferred_element_type=jnp.float32)


def kernel(
    subs, levels, noise_hbm, block_hbm, proj_hbm, expand_hbm, out,
    noise, low, gat, blk, proj, expand, acc, parts, got_a, chip, chip_b, got_b, run, got_c, co,
    ld, ld_blk, own_s, own_r, x_s, x_r, f_s, a_s, a_r, b_s, b_r, c_s, c_r, d_s, d_r, near_sem,
):
    chips = subs // 2
    chunks, vecs, kc = gat.shape[1:]
    points = chunks * kc
    rank = proj.shape[1]
    half = rank // 2
    tiles, _, tile = acc.shape
    me = lax.axis_index("sub")
    leaf = lax.axis_index("leaf")
    core = lax.rem(me, 2)
    x = me // 2
    mate = me + 1 - 2 * core

    def chip_at(d):
        return lax.rem(x + d, chips)

    def chip_from(d):
        return lax.rem(x + chips - d, chips)

    def leaf_mate(level):
        bit = lax.rem(leaf // 2**level, 2)
        return leaf + 2**level * (1 - 2 * bit)

    def remote(src, dst, send, recv, **device):
        return pltpu.make_async_remote_copy(
            src_ref=src, dst_ref=dst, send_sem=send, recv_sem=recv, device_id=device, device_id_type=MESH
        )

    loads = [
        pltpu.make_async_copy(noise_hbm, noise, ld.at[0]),
        pltpu.make_async_copy(proj_hbm, proj, ld.at[1]),
        pltpu.make_async_copy(expand_hbm, expand, ld.at[2]),
    ]

    def load_blk(j):
        columns = pl.ds(pl.multiple_of(j * points, points), points)
        return pltpu.make_async_copy(block_hbm.at[0, :, columns], blk.at[j], ld_blk.at[j])

    leaves = lax.axis_size("leaf")

    def beside(act):
        @pl.when(leaf > 0)
        def _():
            act(leaf - 1, 0)

        @pl.when(leaf < leaves - 1)
        def _():
            act(leaf + 1, 1)

    def tell(turn):
        beside(
            lambda at, side: pl.semaphore_signal(
                near_sem.at[1 - side, turn], inc=1, device_id={"leaf": at}, device_id_type=MESH
            )
        )

    def hear(turn):
        beside(lambda at, side: pl.semaphore_wait(near_sem.at[side, turn], 1))

    barrier = pltpu.get_barrier_semaphore()
    pl.semaphore_signal(barrier, inc=1, device_id={"sub": mate}, device_id_type=MESH)
    for d in range(1, chips):
        pl.semaphore_signal(barrier, inc=1, device_id={"sub": chip_at(d) * 2 + core}, device_id_type=MESH)
    beside(lambda at, side: pl.semaphore_signal(barrier, inc=1, device_id={"leaf": at}, device_id_type=MESH))

    loads[0].start()
    loads[1].start()
    loads[0].wait()
    loads[1].wait()
    load_blk(me).start()
    load_blk(mate).start()
    loads[2].start()
    for d in range(1, chips):
        for c in (core, 1 - core):
            load_blk(chip_from(d) * 2 + c).start()

    for k in range(chunks):
        piece = noise[:, k * kc : (k + 1) * kc]
        gat[me, k], low[:, k * kc : (k + 1) * kc] = split(piece)

    sends = []

    def go(copy):
        copy.start()
        sends.append(copy)
        return copy

    def near(j, ks, init=False):
        lhs = jnp.concatenate([gat[j, k] for k in ks], axis=1)
        lanes = slice(ks[0] * kc, (ks[-1] + 1) * kc)

        def step(t, _):
            rows = pl.ds(pl.multiple_of(t * tile, tile), tile)
            product = dot(lhs, blk[j, rows, lanes], 1, 1)
            if init:
                acc[t] = product
            else:
                acc[t] += product
            return 0

        lax.fori_loop(0, tiles, step, 0, unroll=True)

    def send_x(k):
        for d in range(1, chips):
            go(remote(gat.at[me, k], gat.at[me, k], x_s.at[d, k], x_r.at[me, k], sub=chip_at(d) * 2 + core))

    high = jnp.concatenate([gat[me, k] for k in range(chunks)], axis=1)
    p_high, p_low = split(proj[...].reshape(levels * rank, points))
    both = dot(jnp.concatenate([p_high, p_low], axis=0), high, 1, 1)
    part = both[: levels * rank] + both[levels * rank :] + dot(p_high, low[...], 1, 1)
    for c in range(2):
        for level in range(levels):
            first = level * rank + c * half
            parts[c, level] = part[first : first + half]

    pl.semaphore_wait(barrier, chips + (leaf + leaves - 1) // leaves + (2 * leaves - 2 - leaf) // leaves)
    if levels > 1:
        tell(0)
    for k in range(EARLY):
        send_x(k)

    a = go(remote(parts.at[1 - core], got_a, a_s, a_r, sub=mate))
    own = go(remote(gat.at[me], gat.at[me], own_s, own_r, sub=mate))

    a.wait_recv()
    chip[...] = parts[core] + got_a[...]
    chip_b[...] = chip[...].astype(jnp.bfloat16)
    for d in range(1, chips):
        go(remote(chip_b, got_b.at[x], b_s.at[d], b_r.at[x], sub=chip_at(d) * 2 + core))
    for k in range(EARLY, chunks):
        send_x(k)

    every = list(range(chunks))
    load_blk(me).wait()
    near(me, every, init=True)
    own.wait_recv()
    load_blk(mate).wait()
    near(mate, every)

    c_copies = {}

    def send_c(level):
        for turn in range(2 ** max(level - 1, 0) - 1, 2**level - 1):
            if turn:
                tell(turn)
            hear(turn)
        more = levels - level - 1
        rows = [(0, pl.ds(level + 1, more))] if more else []
        for which, at in rows + [(1, pl.ds(level, 1))]:
            c_copies[level, which] = go(
                remote(
                    run.at[level, at],
                    got_c.at[level, at],
                    c_s.at[level, which],
                    c_r.at[level, which],
                    leaf=leaf_mate(level),
                )
            )

    def recv_b():
        total = chip[...]
        for d in range(1, chips):
            src = chip_from(d)
            remote(chip_b, got_b.at[src], b_s.at[d], b_r.at[src], sub=mate).wait_recv()
            total = total + got_b[src].astype(jnp.float32)
        run[0] = total
        send_c(0)

    def recv_c(level):
        if level + 1 < levels:
            c_copies[level, 0].wait_recv()
            run[level + 1, level + 1 :] = run[level, level + 1 :] + got_c[level, level + 1 :]
            send_c(level + 1)
        c_copies[level, 1].wait_recv()
        co[core, level] = got_c[level, level]
        go(remote(co.at[core, level], co.at[core, level], d_s.at[level], d_r.at[level], sub=mate))

    slots = {0: [recv_b]}
    for level in range(levels):
        slots.setdefault(max(0, (level + 1) * chunks // levels - 2), []).append(functools.partial(recv_c, level))

    for d in range(1, chips):
        load_blk(chip_from(d) * 2 + core).wait()
        load_blk(chip_from(d) * 2 + 1 - core).wait()

    for k in range(chunks):
        for d in range(1, chips):
            src = chip_from(d) * 2 + core
            remote(gat.at[src, k], gat.at[src, k], x_s.at[d, k], x_r.at[src, k], sub=mate).wait_recv()
            go(remote(gat.at[src, k], gat.at[src, k], f_s.at[d, k], x_r.at[src, k], sub=mate))
        for event in slots.get(k, []):
            event()
        for d in range(1, chips):
            near(chip_from(d) * 2 + core, [k])
        if k == chunks - 1:
            break
        for d in range(1, chips):
            src = chip_from(d) * 2 + 1 - core
            remote(gat.at[src, k], gat.at[src, k], x_s.at[d, k], x_r.at[src, k], sub=mate).wait_recv()
            near(src, [k])

    for level in range(levels):
        other = co.at[1 - core, level]
        remote(other, other, d_s.at[level], d_r.at[level], sub=mate).wait_recv()
    loads[2].wait()
    coeff = jnp.concatenate([co[c, level] for level in range(levels) for c in range(2)], axis=0)
    c_high, c_low = split(coeff)
    lhs = jnp.concatenate([c_high, c_high, c_low], axis=0)
    for t in range(tiles):
        e_high, e_low = split(expand[:, :, t * tile : (t + 1) * tile].reshape(levels * rank, tile))
        acc[t] += dot(lhs, jnp.concatenate([e_high, e_low, e_high], axis=0), 0, 0)

    k = chunks - 1
    for d in range(1, chips):
        src = chip_from(d) * 2 + 1 - core
        remote(gat.at[src, k], gat.at[src, k], x_s.at[d, k], x_r.at[src, k], sub=mate).wait_recv()
    for t in range(tiles):
        total = acc[t]
        for d in range(1, chips):
            src = chip_from(d) * 2 + 1 - core
            total = total + dot(gat[src, k], blk[src, t * tile : (t + 1) * tile, k * kc : (k + 1) * kc], 1, 1)
        out[:, t * tile : (t + 1) * tile] = total

    for copy in sends:
        copy.wait_send()


def solution(mesh):
    subs = mesh.shape["sub"]
    chips = subs // 2

    def shards(noise, leaf_blocks, proj_basis, expand_basis):
        vecs, points = noise.shape
        levels, rank = proj_basis.shape[:2]
        chunks = CHUNKS if points // CHUNKS >= 128 else points // 128
        kc = points // chunks
        tile = min(TILE, points)
        tiles = points // tile
        f32, bf16 = jnp.float32, jnp.bfloat16
        dma = pltpu.SemaphoreType.DMA
        part = (levels, rank // 2, vecs)
        return pl.pallas_call(
            functools.partial(kernel, subs, levels),
            out_shape=pltpu.VMEM((vecs, points), f32),
            in_specs=[pl.BlockSpec(memory_space=pltpu.HBM)] * 4,
            out_specs=pl.BlockSpec(memory_space=pltpu.VMEM),
            scratch_shapes=[
                pltpu.VMEM((vecs, points), f32),
                pltpu.VMEM((vecs, points), bf16),
                pltpu.VMEM((subs, chunks, vecs, kc), bf16),
                pltpu.VMEM((subs, points, points), bf16),
                pltpu.VMEM((levels, rank, points), f32),
                pltpu.VMEM((levels, rank, points), f32),
                pltpu.VMEM((tiles, vecs, tile), f32),
                pltpu.VMEM((2,) + part, f32),
                pltpu.VMEM(part, f32),
                pltpu.VMEM(part, f32),
                pltpu.VMEM(part, bf16),
                pltpu.VMEM((chips,) + part, bf16),
                pltpu.VMEM((levels,) + part, f32),
                pltpu.VMEM((levels,) + part, f32),
                pltpu.VMEM((2,) + part, f32),
                dma((3,)),
                dma((subs,)),
                dma, dma,
                dma((chips, chunks)),
                dma((subs, chunks)),
                dma((chips, chunks)),
                dma, dma,
                dma((chips,)),
                dma((chips,)),
                dma((levels, 2)),
                dma((levels, 2)),
                dma((levels,)),
                dma((levels,)),
                pltpu.SemaphoreType.REGULAR((2, 2**levels)),
            ],
            compiler_params=pltpu.CompilerParams(
                collective_id=0, has_side_effects=True, vmem_limit_bytes=LIMIT
            ),
        )(noise, leaf_blocks, proj_basis, expand_basis)

    return jax.shard_map(
        shards,
        mesh=mesh,
        in_specs=(
            P("groups", ("leaf", "sub")),
            P(("groups", "leaf"), "sub", None),
            P("groups", None, ("leaf", "sub")),
            P("groups", None, ("leaf", "sub")),
        ),
        out_specs=P("groups", ("leaf", "sub")),
        check_vma=False,
    )
```

```python
import functools

import jax
import jax.numpy as jnp
from jax import lax
from jax.experimental import pallas as pl
from jax.experimental.pallas import tpu as pltpu
from jax.sharding import PartitionSpec as P

MESH = pl.DeviceIdType.MESH
CHUNKS = 8
EARLY = 1
TILE = 256
LIMIT = 61 * 2**20


def split(value):
    high = value.astype(jnp.bfloat16)
    return high, (value - high.astype(jnp.float32)).astype(jnp.bfloat16)


def dot(a, b, da, db):
    return lax.dot_general(a, b, (((da,), (db,)), ((), ())), preferred_element_type=jnp.float32)


def kernel(
    subs, levels, noise_hbm, block_hbm, proj_hbm, expand_hbm, out,
    noise, low, gat, blk, proj, expand, acc, parts, got_a, chip, chip_b, got_b, run, got_c, co,
    ld, ld_blk, own_s, own_r, x_s, x_r, f_s, a_s, a_r, b_s, b_r, c_s, c_r, d_s, d_r, near_sem,
):
    chips = subs // 2
    chunks, vecs, kc = gat.shape[1:]
    points = chunks * kc
    rank = proj.shape[1]
    half = rank // 2
    tiles, _, tile = acc.shape
    me = lax.axis_index("sub")
    leaf = lax.axis_index("leaf")
    core = lax.rem(me, 2)
    x = me // 2
    mate = me + 1 - 2 * core

    def chip_at(d):
        return lax.rem(x + d, chips)

    def chip_from(d):
        return lax.rem(x + chips - d, chips)

    def leaf_mate(level):
        bit = lax.rem(leaf // 2**level, 2)
        return leaf + 2**level * (1 - 2 * bit)

    def remote(src, dst, send, recv, **device):
        return pltpu.make_async_remote_copy(
            src_ref=src, dst_ref=dst, send_sem=send, recv_sem=recv, device_id=device, device_id_type=MESH
        )

    loads = [
        pltpu.make_async_copy(noise_hbm, noise, ld.at[0]),
        pltpu.make_async_copy(proj_hbm, proj, ld.at[1]),
        pltpu.make_async_copy(expand_hbm, expand, ld.at[2]),
    ]

    def load_blk(j):
        columns = pl.ds(pl.multiple_of(j * points, points), points)
        return pltpu.make_async_copy(block_hbm.at[0, :, columns], blk.at[j], ld_blk.at[j])

    leaves = lax.axis_size("leaf")

    def beside(act):
        @pl.when(leaf > 0)
        def _():
            act(leaf - 1, 0)

        @pl.when(leaf < leaves - 1)
        def _():
            act(leaf + 1, 1)

    def tell(turn):
        beside(
            lambda at, side: pl.semaphore_signal(
                near_sem.at[1 - side, turn], inc=1, device_id={"leaf": at}, device_id_type=MESH
            )
        )

    def hear(turn):
        beside(lambda at, side: pl.semaphore_wait(near_sem.at[side, turn], 1))

    barrier = pltpu.get_barrier_semaphore()
    pl.semaphore_signal(barrier, inc=1, device_id={"sub": mate}, device_id_type=MESH)
    for d in range(1, chips):
        pl.semaphore_signal(barrier, inc=1, device_id={"sub": chip_at(d) * 2 + core}, device_id_type=MESH)
    beside(lambda at, side: pl.semaphore_signal(barrier, inc=1, device_id={"leaf": at}, device_id_type=MESH))

    loads[0].start()
    loads[1].start()
    loads[0].wait()
    loads[1].wait()
    load_blk(me).start()
    load_blk(mate).start()
    loads[2].start()
    for d in range(1, chips):
        for c in (core, 1 - core):
            load_blk(chip_from(d) * 2 + c).start()

    for k in range(chunks):
        piece = noise[:, k * kc : (k + 1) * kc]
        gat[me, k], low[:, k * kc : (k + 1) * kc] = split(piece)

    sends = []

    def go(copy):
        copy.start()
        sends.append(copy)
        return copy

    def near(j, ks, init=False):
        lhs = jnp.concatenate([gat[j, k] for k in ks], axis=1)
        lanes = slice(ks[0] * kc, (ks[-1] + 1) * kc)

        def step(t, _):
            rows = pl.ds(pl.multiple_of(t * tile, tile), tile)
            product = dot(lhs, blk[j, rows, lanes], 1, 1)
            if init:
                acc[t] = product
            else:
                acc[t] += product
            return 0

        lax.fori_loop(0, tiles, step, 0, unroll=True)

    def send_x(k):
        for d in range(1, chips):
            go(remote(gat.at[me, k], gat.at[me, k], x_s.at[d, k], x_r.at[me, k], sub=chip_at(d) * 2 + core))

    high = jnp.concatenate([gat[me, k] for k in range(chunks)], axis=1)
    p_high, p_low = split(proj[...].reshape(levels * rank, points))
    both = dot(jnp.concatenate([p_high, p_low], axis=0), high, 1, 1)
    part = both[: levels * rank] + both[levels * rank :] + dot(p_high, low[...], 1, 1)
    for c in range(2):
        for level in range(levels):
            first = level * rank + c * half
            parts[c, level] = part[first : first + half]

    pl.semaphore_wait(barrier, chips + (leaf + leaves - 1) // leaves + (2 * leaves - 2 - leaf) // leaves)
    if levels > 1:
        tell(0)
    for k in range(EARLY):
        send_x(k)

    a = go(remote(parts.at[1 - core], got_a, a_s, a_r, sub=mate))
    own = go(remote(gat.at[me], gat.at[me], own_s, own_r, sub=mate))

    a.wait_recv()
    chip[...] = parts[core] + got_a[...]
    chip_b[...] = chip[...].astype(jnp.bfloat16)
    for d in range(1, chips):
        for level in reversed(range(levels)):
            go(
                remote(
                    chip_b.at[level], got_b.at[x, level], b_s.at[d, level], b_r.at[x, level], sub=chip_at(d) * 2 + core
                )
            )
    for k in range(EARLY, chunks):
        send_x(k)

    every = list(range(chunks))
    load_blk(me).wait()
    near(me, every, init=True)
    own.wait_recv()
    load_blk(mate).wait()
    near(mate, every)

    c_copies = {}

    def send_c(level, kinds=(0, 1)):
        for turn in range(2 ** max(level - 1, 0) - 1, 2**level - 1):
            if turn:
                tell(turn)
            hear(turn)
        more = levels - level - 1
        rows = [(0, pl.ds(level + 1, more))] if more else []
        for which, at in rows + [(1, pl.ds(level, 1))]:
            if which not in kinds:
                continue
            c_copies[level, which] = go(
                remote(
                    run.at[level, at],
                    got_c.at[level, at],
                    c_s.at[level, which],
                    c_r.at[level, which],
                    leaf=leaf_mate(level),
                )
            )

    def recv_b():
        for level in reversed(range(levels)):
            total = chip[level]
            for d in range(1, chips):
                src = chip_from(d)
                remote(
                    chip_b.at[level], got_b.at[src, level], b_s.at[d, level], b_r.at[src, level], sub=mate
                ).wait_recv()
                total = total + got_b[src, level].astype(jnp.float32)
            run[0, level] = total
            if level == 1:
                send_c(0, (0,))
        send_c(0, (1,))

    def recv_c(level):
        if level + 1 < levels:
            c_copies[level, 0].wait_recv()
            run[level + 1, level + 1 :] = run[level, level + 1 :] + got_c[level, level + 1 :]
            send_c(level + 1)
        c_copies[level, 1].wait_recv()
        co[core, level] = got_c[level, level]
        go(remote(co.at[core, level], co.at[core, level], d_s.at[level], d_r.at[level], sub=mate))

    slots = {0: [recv_b]}
    for level in range(levels):
        slots.setdefault(max(0, (level + 1) * chunks // levels - 2), []).append(functools.partial(recv_c, level))

    for d in range(1, chips):
        load_blk(chip_from(d) * 2 + core).wait()
        load_blk(chip_from(d) * 2 + 1 - core).wait()

    for k in range(chunks):
        for d in range(1, chips):
            src = chip_from(d) * 2 + core
            remote(gat.at[src, k], gat.at[src, k], x_s.at[d, k], x_r.at[src, k], sub=mate).wait_recv()
            go(remote(gat.at[src, k], gat.at[src, k], f_s.at[d, k], x_r.at[src, k], sub=mate))
        for event in slots.get(k, []):
            event()
        for d in range(1, chips):
            near(chip_from(d) * 2 + core, [k])
        if k == chunks - 1:
            break
        for d in range(1, chips):
            src = chip_from(d) * 2 + 1 - core
            remote(gat.at[src, k], gat.at[src, k], x_s.at[d, k], x_r.at[src, k], sub=mate).wait_recv()
            near(src, [k])

    for level in range(levels):
        other = co.at[1 - core, level]
        remote(other, other, d_s.at[level], d_r.at[level], sub=mate).wait_recv()
    loads[2].wait()
    coeff = jnp.concatenate([co[c, level] for level in range(levels) for c in range(2)], axis=0)
    c_high, c_low = split(coeff)
    lhs = jnp.concatenate([c_high, c_high, c_low], axis=0)
    for t in range(tiles):
        e_high, e_low = split(expand[:, :, t * tile : (t + 1) * tile].reshape(levels * rank, tile))
        acc[t] += dot(lhs, jnp.concatenate([e_high, e_low, e_high], axis=0), 0, 0)

    k = chunks - 1
    for d in range(1, chips):
        src = chip_from(d) * 2 + 1 - core
        remote(gat.at[src, k], gat.at[src, k], x_s.at[d, k], x_r.at[src, k], sub=mate).wait_recv()
    for t in range(tiles):
        total = acc[t]
        for d in range(1, chips):
            src = chip_from(d) * 2 + 1 - core
            total = total + dot(gat[src, k], blk[src, t * tile : (t + 1) * tile, k * kc : (k + 1) * kc], 1, 1)
        out[:, t * tile : (t + 1) * tile] = total

    for copy in sends:
        copy.wait_send()


def solution(mesh):
    subs = mesh.shape["sub"]
    chips = subs // 2

    def shards(noise, leaf_blocks, proj_basis, expand_basis):
        vecs, points = noise.shape
        levels, rank = proj_basis.shape[:2]
        chunks = CHUNKS if points // CHUNKS >= 128 else points // 128
        kc = points // chunks
        tile = min(TILE, points)
        tiles = points // tile
        f32, bf16 = jnp.float32, jnp.bfloat16
        dma = pltpu.SemaphoreType.DMA
        part = (levels, rank // 2, vecs)
        return pl.pallas_call(
            functools.partial(kernel, subs, levels),
            out_shape=pltpu.VMEM((vecs, points), f32),
            in_specs=[pl.BlockSpec(memory_space=pltpu.HBM)] * 4,
            out_specs=pl.BlockSpec(memory_space=pltpu.VMEM),
            scratch_shapes=[
                pltpu.VMEM((vecs, points), f32),
                pltpu.VMEM((vecs, points), bf16),
                pltpu.VMEM((subs, chunks, vecs, kc), bf16),
                pltpu.VMEM((subs, points, points), bf16),
                pltpu.VMEM((levels, rank, points), f32),
                pltpu.VMEM((levels, rank, points), f32),
                pltpu.VMEM((tiles, vecs, tile), f32),
                pltpu.VMEM((2,) + part, f32),
                pltpu.VMEM(part, f32),
                pltpu.VMEM(part, f32),
                pltpu.VMEM(part, bf16),
                pltpu.VMEM((chips,) + part, bf16),
                pltpu.VMEM((levels,) + part, f32),
                pltpu.VMEM((levels,) + part, f32),
                pltpu.VMEM((2,) + part, f32),
                dma((3,)),
                dma((subs,)),
                dma, dma,
                dma((chips, chunks)),
                dma((subs, chunks)),
                dma((chips, chunks)),
                dma, dma,
                dma((chips, levels)),
                dma((chips, levels)),
                dma((levels, 2)),
                dma((levels, 2)),
                dma((levels,)),
                dma((levels,)),
                pltpu.SemaphoreType.REGULAR((2, 2**levels)),
            ],
            compiler_params=pltpu.CompilerParams(
                collective_id=0, has_side_effects=True, vmem_limit_bytes=LIMIT
            ),
        )(noise, leaf_blocks, proj_basis, expand_basis)

    return jax.shard_map(
        shards,
        mesh=mesh,
        in_specs=(
            P("groups", ("leaf", "sub")),
            P(("groups", "leaf"), "sub", None),
            P("groups", None, ("leaf", "sub")),
            P("groups", None, ("leaf", "sub")),
        ),
        out_specs=P("groups", ("leaf", "sub")),
        check_vma=False,
    )
```
